32 devices in a mesh: domain: 8 (over z, x), band: 4 (over y, core).
Axes of the slice: x: 2, y: 2, z: 4, core: 2. Of those that a mesh axis runs over, the one named last changes fastest.
Arguments:
- wavefunctions: bfloat16 [32000, 1024], P('domain', 'band'), may hold values from -6 to 6
- potential: float32 [32000], P('domain'), may hold values from -1.5 to 0.5
- cell_matrix: bfloat16 [125, 125], replicated, may hold values from -0.5 to 0.5
- neighbours: int32 [256, 6], P('domain'), may hold values from 0 to 63, as said below
- window: float32 [2], replicated, may hold values from -1.6 to 5.6, as said below
Outputs:
- filtered: bfloat16 [32000, 1024], P('domain', 'band')
- projected: float32 [1024, 1024], P('band')
The draws below stay inside these ranges and needn't reach their ends.
Inputs may be any that keep to these rules, and one draw needn't show every extreme that they name: `neighbours`: the cells form a periodic grid of 4 x 4 x (16) cells, domain g holding z layers g * 2 to g * 2 + 1; slots 0 to 15 of a domain are its lowest layer and the last 16 slots its highest, in a drawn order, the rest in a drawn order. Entries follow the meaning stated in the reference program; values of 32 or more stand only in the -z column of the lowest layer and the +z column of the highest. Faces pair up: if cell a meets cell b across face d, b meets a across d xor 1. window[0] < window[1], and every eigenvalue of H lies below window[1].
All inputs are finite; a program needn't handle non-finite values.
Results may differ from the reference program's by a relative error of at most 0.01.
The reference program's roundings to bfloat16 on the way count: a program that leaves them out, or rounds other values in their place, can miss the bound.
Values may be sent and summed in bfloat16 or wider, within the bound.
A program may use at most 128 MiB of HBM per device.

```python
import jax
import jax.numpy as jnp
from jax import lax

NWF = 1024
NPC = 125
SIDE = 4
LAYERS = 2
CELLS_DEV = 32
NODES = 32000
N_DOMAIN = 8


def shared_modes(key, weight):
    total = jnp.zeros((NODES, NWF), jnp.float32)
    for term in range(4):
        signs = jax.random.rademacher(jax.random.fold_in(key, 100 + term), (NODES, 1)).astype(jnp.float32)
        column_weights = jnp.clip(jax.random.normal(jax.random.fold_in(key, 200 + term), (1, NWF), jnp.float32), -3.0, 3.0)
        total = total + weight * signs * column_weights
    return total


def draw_wavefunctions(key, part):
    key = jax.random.fold_in(key, 7)
    noise_key = jax.random.fold_in(key, 31)
    noise = jax.random.normal(noise_key, (NODES, NWF), jnp.float32)
    values = noise + shared_modes(key, 0.3)
    return jnp.clip(values, -6.0, 6.0).astype(jnp.bfloat16)


def draw_neighbours(key, part):
    face_cells = SIDE * SIDE
    cell_count = face_cells * LAYERS

    def arrange(subkey):
        pieces = [jax.random.permutation(jax.random.fold_in(subkey, 11), face_cells)]
        if LAYERS > 2:
            pieces.append(jax.random.permutation(jax.random.fold_in(subkey, 17), face_cells * (LAYERS - 2)) + face_cells)
        pieces.append(jax.random.permutation(jax.random.fold_in(subkey, 13), face_cells) + (LAYERS - 1) * face_cells)
        return jnp.concatenate(pieces).astype(jnp.int32)
    position = jax.vmap(arrange)(jax.random.split(jax.random.fold_in(key, 5), N_DOMAIN))
    slot_at = jnp.argsort(position, axis=1).astype(jnp.int32)
    level = position // face_cells
    across = position % face_cells // SIDE
    along = position % SIDE

    def local_slot(level_index, across_index, along_index):
        return jnp.take_along_axis(slot_at, level_index * face_cells + across_index * SIDE + along_index, axis=1)
    minus_x = local_slot(level, (across - 1) % SIDE, along)
    plus_x = local_slot(level, (across + 1) % SIDE, along)
    minus_y = local_slot(level, across, (along - 1) % SIDE)
    plus_y = local_slot(level, across, (along + 1) % SIDE)
    below_slot = jnp.take_along_axis(jnp.roll(slot_at, 1, axis=0), (LAYERS - 1) * face_cells + across * SIDE + along, axis=1) - (cell_count - face_cells) + cell_count
    minus_z = jnp.where(level > 0, local_slot(jnp.maximum(level - 1, 0), across, along), below_slot)
    above_slot = jnp.take_along_axis(jnp.roll(slot_at, -1, axis=0), across * SIDE + along, axis=1) + cell_count + face_cells
    plus_z = jnp.where(level < LAYERS - 1, local_slot(jnp.minimum(level + 1, LAYERS - 1), across, along), above_slot)
    stacked = jnp.stack([minus_x, plus_x, minus_y, plus_y, minus_z, plus_z], axis=-1)
    return stacked.reshape(N_DOMAIN * cell_count, 6).astype(jnp.int32)


def draw_window(key, part):
    lower_key = jax.random.fold_in(key, 21)
    upper_key = jax.random.fold_in(key, 23)
    bottom = jax.random.uniform(lower_key, (), jnp.float32, -1.5, -1.3)
    ceiling = jax.random.uniform(upper_key, (), jnp.float32, 5.1, 5.4)
    return jnp.stack([bottom, ceiling]).astype(jnp.float32)


def block_levels(rng, dims, shards, least, top_value):
    def one(dim, parts):
        draws = jax.random.uniform(jax.random.fold_in(jax.random.fold_in(rng, 6), dim), (parts,), jnp.float32, least / len(shards), top_value / len(shards))
        return jnp.repeat(jnp.exp(draws), dims[dim] // parts).reshape((-1,) + (1,) * (len(dims) - dim - 1))

    factor_of = one(*shards[0])
    for cut in shards[1:]:
        factor_of = factor_of * one(*cut)
    return factor_of


def scatter_about(rng, extent, width, limit, held_as=jnp.bfloat16):
    entries = width * jax.random.normal(rng, extent, jnp.float32)
    return jnp.clip(entries, min=-limit, max=limit).astype(held_as)


def setup_inputs(seed: int = 0) -> dict:
    streams_of = jax.random.split(jax.random.key(seed), 6)
    wavefunctions = draw_wavefunctions(jax.random.fold_in(streams_of[5], 71), 0)
    potential = jnp.clip(-1.5 + 2.0 * jax.random.uniform(streams_of[1], (NODES,), jnp.float32) ** block_levels(streams_of[1], (NODES,), ((0, 8),), -0.2, 0.2), -1.5, 0.5)
    cell_matrix = scatter_about(streams_of[2], (NPC, NPC), NPC ** -0.5, 0.5)
    neighbours = draw_neighbours(jax.random.fold_in(streams_of[5], 71), 0)
    window = draw_window(jax.random.fold_in(streams_of[5], 71), 0)
    return {"wavefunctions": wavefunctions, "potential": potential, "cell_matrix": cell_matrix, "neighbours": neighbours, "window": window}


penalty = 0.5
highest = lax.Precision.HIGHEST

def face_view(field, direction):
    return lax.index_in_dim(field, 4 * (direction % 2), 1 + direction // 2, keepdims=False)

def face_add(field, direction, update):
    position = (slice(None),) * (1 + direction // 2) + (4 * (direction % 2),)
    return field.at[position].add(update)

def apply_block(values, stiffness, local_potential, local_neighbours, from_below, from_above):
    cell_count = local_neighbours.shape[0]
    columns = values.shape[1]
    shaped = values.reshape(cell_count, 5, 5, 5, columns)
    result = jnp.einsum('mn,cnb->cmb', stiffness.astype(jnp.float32), values.reshape(cell_count, NPC, columns).astype(jnp.float32), precision=highest)
    result = result.reshape(cell_count, 5, 5, 5, columns) + local_potential.reshape(cell_count, 5, 5, 5, 1) * shaped.astype(jnp.float32)
    for direction in range(6):
        table = jnp.concatenate([face_view(shaped, direction ^ 1), from_below, from_above], axis=0)
        nearby = jnp.take(table, local_neighbours[:, direction], axis=0)
        result = face_add(result, direction, penalty * (face_view(shaped, direction).astype(jnp.float32) - nearby.astype(jnp.float32)))
    return result.reshape(cell_count * NPC, columns)

def reference(wavefunctions, potential, cell_matrix, neighbours, window):
    wide = cell_matrix.astype(jnp.float32)
    stiffness = ((wide + wide.T) * 0.5).astype(jnp.bfloat16)
    face_cells = SIDE * SIDE

    def operate(values):
        shaped = values.reshape(N_DOMAIN, CELLS_DEV, 5, 5, 5, NWF)
        lower_rims = jnp.roll(shaped[:, CELLS_DEV - face_cells:, :, :, 4], 1, axis=0)
        upper_rims = jnp.roll(shaped[:, :face_cells, :, :, 0], -1, axis=0)

        def one_domain(domain_items):
            domain_block, domain_potential, domain_neighbours, below_rim, above_rim = domain_items
            return apply_block(domain_block, stiffness, domain_potential, domain_neighbours, below_rim, above_rim)
        result = lax.map(one_domain, (values.reshape(N_DOMAIN, CELLS_DEV * NPC, NWF), potential.reshape(N_DOMAIN, CELLS_DEV * NPC), neighbours.reshape(N_DOMAIN, CELLS_DEV, 6), lower_rims, upper_rims))
        return result.reshape(NODES, NWF)
    center = (window[0] + window[1]) * 0.5
    half = (window[1] - window[0]) * 0.5
    image = operate(wavefunctions)
    previous = wavefunctions
    current = ((image - center * wavefunctions.astype(jnp.float32)) / half).astype(jnp.bfloat16)
    for degree in range(3):
        image = operate(current)
        following = (2.0 * (image - center * current.astype(jnp.float32)) / half - previous.astype(jnp.float32)).astype(jnp.bfloat16)
        previous, current = (current, following)
    image_last = operate(current).astype(jnp.bfloat16)
    contract = (((0,), (0,)), ((), ()))
    margin = lax.dot_general(current.astype(jnp.float32), current.astype(jnp.float32), contract, preferred_element_type=jnp.float32) / NODES
    cross = lax.dot_general(current.astype(jnp.float32), image_last.astype(jnp.float32), contract, preferred_element_type=jnp.float32) / NODES
    lower = jnp.linalg.cholesky(margin)
    inverse = jax.scipy.linalg.solve_triangular(lower, jnp.eye(NWF, dtype=jnp.float32), lower=True)
    filtered = lax.dot_general(current.astype(jnp.float32), inverse.astype(jnp.bfloat16).astype(jnp.float32), (((1,), (1,)), ((), ())), preferred_element_type=jnp.float32).astype(jnp.bfloat16)
    left = jnp.dot(inverse.astype(jnp.float32), cross.astype(jnp.float32), precision=highest, preferred_element_type=jnp.float32)
    projected = lax.dot_general(left.astype(jnp.float32), inverse.astype(jnp.float32), (((1,), (1,)), ((), ())), precision=highest, preferred_element_type=jnp.float32)
    return (filtered, projected)
```

```python
import functools

import jax
import jax.numpy as jnp
import numpy as np
from jax import lax
from jax.experimental import pallas as pl
from jax.experimental.pallas import tpu as pltpu
from jax.sharding import PartitionSpec as P

NPC = 125
ROWS = 128
FACE = 32
GROUP = 4
BLOCK = 128
penalty = 0.5
highest = lax.Precision.HIGHEST
MESH = pl.DeviceIdType.MESH


def face_table():
    incidence = np.zeros((ROWS, 6 * FACE), np.float32)
    for direction in range(6):
        axis_index = direction // 2
        level = 4 * (direction % 2)
        for first in range(5):
            for second in range(5):
                others = [first, second]
                coords = others[:axis_index] + [level] + others[axis_index:]
                node = 25 * coords[0] + 5 * coords[1] + coords[2]
                incidence[node, FACE * direction + 5 * first + second] = 1.0
    return incidence


def chain_kernel(steps, plain, count, half_cells, *refs):
    nb_ref, coef_ref, start_ref, weight_ref, comb_ref, pick_ref, out_ref = refs[:7]
    rest = list(refs[7:])
    fields = [start_ref] + rest[: steps - 1] + [out_ref]
    rest = rest[steps - 1 :]
    faces, below, above = rest[:steps], rest[steps : 2 * steps], rest[2 * steps : 3 * steps]
    send_sem, recv_sem = rest[3 * steps :]
    me = lax.axis_index("domain")
    up, down = lax.rem(me + 1, count), lax.rem(me + count - 1, count)

    barrier = pltpu.get_barrier_semaphore()
    for other in (down, up):
        pl.semaphore_signal(barrier, inc=1, device_id={"domain": other}, device_id_type=MESH)
    pl.semaphore_wait(barrier, 2)

    def copy_of(step, part):
        return pltpu.make_async_remote_copy(
            src_ref=faces[step].at[4 + part, pl.ds(half_cells * part, half_cells)],
            dst_ref=(below if part else above)[step],
            send_sem=send_sem.at[step, part],
            recv_sem=recv_sem.at[step, part],
            device_id={"domain": up if part else down},
            device_id_type=MESH,
        )

    def store_faces(step, cell, value):
        picked = jnp.dot(pick_ref[...], value, preferred_element_type=jnp.float32)
        picked = picked.astype(jnp.bfloat16)
        for d in range(6):
            faces[step][d, cell] = picked[FACE * d : FACE * (d + 1)]

    center = coef_ref[0]

    def work(step, part):
        scale = 1.0 if plain else coef_ref[1 if step == 0 else 2]
        shift = 0.0 if plain else center
        now, later = fields[step], fields[step + 1]
        before = fields[step - 1] if step > 0 else None

        def body(index, carry):
            for inner in range(GROUP):
                cell = half_cells * part + index * GROUP + inner
                value = now[cell]
                pieces = [value]
                for d in range(6):
                    slot = nb_ref[cell, d]
                    if d == 4 and part == 0:
                        pieces.append(below[step][lax.rem(slot, half_cells)])
                    elif d == 5 and part == 1:
                        pieces.append(above[step][lax.rem(slot, half_cells)])
                    else:
                        pieces.append(faces[step][d ^ 1, slot])
                stacked = jnp.concatenate(pieces, axis=0)
                image = jnp.dot(comb_ref[...], stacked, preferred_element_type=jnp.float32)
                wide = value.astype(jnp.float32)
                if plain:
                    image = image + weight_ref[cell] * wide
                else:
                    image = image * scale + ((weight_ref[cell] - shift) * scale) * wide
                if before is not None:
                    image = image - before[cell].astype(jnp.float32)
                result = image.astype(jnp.bfloat16)
                later[cell] = result
                if step + 1 < steps:
                    store_faces(step + 1, cell, result)
            return carry

        lax.fori_loop(0, half_cells // GROUP, body, 0)

    def first_faces(part):
        def body(index, carry):
            for inner in range(GROUP):
                cell = half_cells * part + index * GROUP + inner
                store_faces(0, cell, start_ref[cell])
            return carry

        lax.fori_loop(0, half_cells // GROUP, body, 0)

    for part in (0, 1):
        first_faces(part)
        copy_of(0, part).start()
    order = (1, 0)
    for step in range(steps):
        for part in order:
            copy_of(step, 1 - part).wait_recv()
            work(step, part)
            if step + 1 < steps:
                copy_of(step + 1, part).start()
        order = order[::-1]
    for step in range(steps):
        for part in (0, 1):
            copy_of(step, part).wait_send()


def chain(start, neighbours, coefs, weight, comb, pick, steps, plain, ident):
    count = lax.axis_size("domain")
    cells, _, columns = start.shape
    half_cells = cells // 2
    vmem = pl.BlockSpec(memory_space=pltpu.VMEM)
    smem = pl.BlockSpec(memory_space=pltpu.SMEM)
    field = pltpu.VMEM(start.shape, jnp.bfloat16)
    rim = pltpu.VMEM((half_cells, FACE, columns), jnp.bfloat16)
    return pl.pallas_call(
        functools.partial(chain_kernel, steps, plain, count, half_cells),
        out_shape=jax.ShapeDtypeStruct(start.shape, jnp.bfloat16),
        in_specs=[smem, smem, vmem, vmem, vmem, vmem],
        out_specs=vmem,
        scratch_shapes=[field] * (steps - 1)
        + [pltpu.VMEM((6, cells, FACE, columns), jnp.bfloat16)] * steps
        + [rim] * (2 * steps)
        + [pltpu.SemaphoreType.DMA((steps, 2)), pltpu.SemaphoreType.DMA((steps, 2))],
        compiler_params=pltpu.CompilerParams(
            collective_id=ident, has_side_effects=True, vmem_limit_bytes=48 * 2**20
        ),
        cost_estimate=pl.CostEstimate(
            flops=steps * cells * 2 * columns * ROWS * 512,
            bytes_accessed=steps * 16 * 2**20,
            transcendentals=0,
        ),
        name="chain" if not plain else "image",
    )(neighbours, coefs, start, weight, comb, pick)


def factor_inverse(block):
    lanes = lax.broadcasted_iota(jnp.int32, (8, BLOCK), 1)
    subs = lax.broadcasted_iota(jnp.int32, (8, BLOCK), 0)
    tiles = [block[8 * t : 8 * t + 8] for t in range(BLOCK // 8)]
    done = [jnp.zeros((8, BLOCK), jnp.float32) for _ in tiles]
    for j in range(BLOCK):
        at, within = divmod(j, 8)
        row = jnp.broadcast_to(tiles[at][within : within + 1], (8, BLOCK))
        pivot = jnp.broadcast_to(row[:, j : j + 1], (8, BLOCK))
        here = lanes == j
        unit = jnp.where(here, 1.0, row)
        scaled = unit * (1.0 / pivot)
        final = jnp.where(lanes <= j, unit, 0.0) * lax.rsqrt(pivot)
        done[at] = jnp.where(subs == within, final, done[at])
        for t in range(at, BLOCK // 8):
            if t == at and within == 7:
                continue
            tile = tiles[t]
            column = jnp.broadcast_to(tile[:, j : j + 1], (8, BLOCK))
            fresh = jnp.where(here, 0.0, tile) - column * scaled
            tiles[t] = jnp.where(subs > within, fresh, tile) if t == at else fresh
    return jnp.concatenate(done, axis=0)


def inverse_kernel(source_ref, out_ref, row_ref):
    size = source_ref.shape[0]
    blocks = size // BLOCK
    out_ref[...] = source_ref[...]
    rows_of = lax.broadcasted_iota(jnp.int32, (BLOCK, BLOCK), 0)
    lanes_of = lax.broadcasted_iota(jnp.int32, (BLOCK, BLOCK), 1)
    eye = (rows_of == lanes_of).astype(jnp.float32)
    column_ids = lax.broadcasted_iota(jnp.int32, (BLOCK, size), 1)

    def step(k, carry):
        base = pl.multiple_of(k * BLOCK, BLOCK)
        own = pl.ds(base, BLOCK)
        small = factor_inverse(out_ref[own, own])
        out_ref[own, own] = eye
        row_ref[...] = jnp.dot(
            small, out_ref[own, :], precision=highest, preferred_element_type=jnp.float32
        )
        out_ref[own, :] = jnp.where(column_ids < base + BLOCK, row_ref[...], 0.0)

        def update(i, inner):
            low = pl.ds(pl.multiple_of(i * BLOCK, BLOCK), BLOCK)
            out_ref[low, own] = jnp.zeros((BLOCK, BLOCK), jnp.float32)
            out_ref[low, :] = out_ref[low, :] - lax.dot_general(
                row_ref[:, low],
                row_ref[...],
                (((0,), (0,)), ((), ())),
                precision=highest,
                preferred_element_type=jnp.float32,
            )
            return inner

        return lax.fori_loop(k + 1, blocks, update, carry)

    lax.fori_loop(0, blocks, step, 0)


def cholesky_inverse(margin):
    size = margin.shape[0]
    return pl.pallas_call(
        inverse_kernel,
        out_shape=jax.ShapeDtypeStruct(margin.shape, jnp.float32),
        in_specs=[pl.BlockSpec(memory_space=pltpu.VMEM)],
        out_specs=pl.BlockSpec(memory_space=pltpu.VMEM),
        scratch_shapes=[pltpu.VMEM((BLOCK, size), jnp.float32)],
        compiler_params=pltpu.CompilerParams(vmem_limit_bytes=40 * 2**20),
        cost_estimate=pl.CostEstimate(
            flops=40 * size**3, bytes_accessed=8 * size * size, transcendentals=size
        ),
        name="cholesky_inverse",
    )(margin)


def per_device(wavefunctions, potential, cell_matrix, neighbours, window):
    cells = neighbours.shape[0]
    nodes, columns = wavefunctions.shape
    wide = cell_matrix.astype(jnp.float32)
    stiffness = ((wide + wide.T) * 0.5).astype(jnp.bfloat16)
    table = face_table()
    pad = ROWS - NPC
    comb = jnp.concatenate(
        [jnp.pad(stiffness, ((0, pad), (0, pad))), jnp.asarray(-penalty * table, jnp.bfloat16)],
        axis=1,
    )
    pick = jnp.asarray(table.T, jnp.bfloat16)
    weight = (
        jnp.pad(potential.reshape(cells, NPC), ((0, 0), (0, pad)))
        + penalty * jnp.asarray(table.sum(axis=1))[None, :]
    )[:, :, None]
    center = (window[0] + window[1]) * 0.5
    half = (window[1] - window[0]) * 0.5
    coefs = jnp.stack([center, 1.0 / half, 2.0 / half])
    start = jnp.pad(wavefunctions.reshape(cells, NPC, columns), ((0, 0), (0, pad), (0, 0)))
    common = (neighbours, coefs, weight, comb, pick)
    last = chain(start, *common, 4, False, 0)
    gathered = lax.all_gather(last.reshape(cells * ROWS, columns), "band", axis=0)
    image = chain(last, *common, 1, True, 1).reshape(cells * ROWS, columns)
    last = last.reshape(cells * ROWS, columns)
    bands = gathered.shape[0]
    size = bands * columns

    margin_part = jnp.einsum(
        "bni,nj->bij", gathered, last, preferred_element_type=jnp.float32
    ).reshape(size, columns)
    cross_part = jnp.einsum(
        "bni,nj->bij", gathered, image, preferred_element_type=jnp.float32
    ).reshape(size, columns)
    total_rows = nodes * lax.axis_size("domain")
    margin_cols = lax.psum(margin_part, "domain")
    cross_cols = lax.psum(cross_part, "domain")
    margin = lax.all_gather(margin_cols.T / total_rows, "band", axis=0, tiled=True)
    cross = lax.all_gather(cross_cols / total_rows, "band", axis=0)
    inverse = cholesky_inverse(margin)
    mine = lax.dynamic_slice_in_dim(inverse, lax.axis_index("band") * columns, columns, 0)
    filtered = jnp.einsum(
        "bnj,kbj->nk",
        gathered,
        mine.astype(jnp.bfloat16).reshape(columns, bands, columns),
        preferred_element_type=jnp.float32,
    ).astype(jnp.bfloat16)
    filtered = filtered.reshape(cells, ROWS, columns)[:, :NPC].reshape(nodes, columns)
    left = jnp.einsum(
        "ik,bkj->ibj", mine, cross, precision=highest, preferred_element_type=jnp.float32
    ).reshape(columns, size)
    projected = lax.dot_general(
        left,
        inverse,
        (((1,), (1,)), ((), ())),
        precision=highest,
        preferred_element_type=jnp.float32,
    )
    return (filtered, projected)


def solution(mesh):
    placed = (P("domain", "band"), P("domain"), P(), P("domain", None), P())
    return jax.shard_map(
        per_device,
        mesh=mesh,
        in_specs=placed,
        out_specs=(P("domain", "band"), P("band", None)),
        check_vma=False,
    )
```

```python
import functools

import jax
import jax.numpy as jnp
import numpy as np
from jax import lax
from jax.experimental import pallas as pl
from jax.experimental.pallas import tpu as pltpu
from jax.sharding import PartitionSpec as P

NPC = 125
ROWS = 128
FACE = 32
GROUP = 4
BLOCK = 128
PIVOTS = 4
penalty = 0.5
highest = lax.Precision.HIGHEST
MESH = pl.DeviceIdType.MESH


def face_table():
    incidence = np.zeros((ROWS, 6 * FACE), np.float32)
    for direction in range(6):
        axis_index = direction // 2
        level = 4 * (direction % 2)
        for first in range(5):
            for second in range(5):
                others = [first, second]
                coords = others[:axis_index] + [level] + others[axis_index:]
                node = 25 * coords[0] + 5 * coords[1] + coords[2]
                incidence[node, FACE * direction + 5 * first + second] = 1.0
    return incidence


def chain_kernel(steps, plain, count, half_cells, *refs):
    nb_ref, coef_ref, start_ref, weight_ref, comb_ref, pick_ref, out_ref = refs[:7]
    rest = list(refs[7:])
    fields = [start_ref] + rest[: steps - 1] + [out_ref]
    rest = rest[steps - 1 :]
    faces, below, above = rest[:steps], rest[steps : 2 * steps], rest[2 * steps : 3 * steps]
    send_sem, recv_sem = rest[3 * steps :]
    me = lax.axis_index("domain")
    up, down = lax.rem(me + 1, count), lax.rem(me + count - 1, count)

    barrier = pltpu.get_barrier_semaphore()
    for other in (down, up):
        pl.semaphore_signal(barrier, inc=1, device_id={"domain": other}, device_id_type=MESH)
    pl.semaphore_wait(barrier, 2)

    def copy_of(step, part):
        return pltpu.make_async_remote_copy(
            src_ref=faces[step].at[4 + part, pl.ds(half_cells * part, half_cells)],
            dst_ref=(below if part else above)[step],
            send_sem=send_sem.at[step, part],
            recv_sem=recv_sem.at[step, part],
            device_id={"domain": up if part else down},
            device_id_type=MESH,
        )

    def store_faces(step, cell, value):
        picked = jnp.dot(pick_ref[...], value, preferred_element_type=jnp.float32)
        picked = picked.astype(jnp.bfloat16)
        for d in range(6):
            faces[step][d, cell] = picked[FACE * d : FACE * (d + 1)]

    center = coef_ref[0]

    def work(step, part):
        scale = 1.0 if plain else coef_ref[1 if step == 0 else 2]
        shift = 0.0 if plain else center
        now, later = fields[step], fields[step + 1]
        before = fields[step - 1] if step > 0 else None

        def body(index, carry):
            for inner in range(GROUP):
                cell = half_cells * part + index * GROUP + inner
                value = now[cell]
                pieces = [value]
                for d in range(6):
                    slot = nb_ref[cell, d]
                    if d == 4 and part == 0:
                        pieces.append(below[step][lax.rem(slot, half_cells)])
                    elif d == 5 and part == 1:
                        pieces.append(above[step][lax.rem(slot, half_cells)])
                    else:
                        pieces.append(faces[step][d ^ 1, slot])
                stacked = jnp.concatenate(pieces, axis=0)
                image = jnp.dot(comb_ref[...], stacked, preferred_element_type=jnp.float32)
                wide = value.astype(jnp.float32)
                if plain:
                    image = image + weight_ref[cell] * wide
                else:
                    image = image * scale + ((weight_ref[cell] - shift) * scale) * wide
                if before is not None:
                    image = image - before[cell].astype(jnp.float32)
                result = image.astype(jnp.bfloat16)
                later[cell] = result
                if step + 1 < steps:
                    store_faces(step + 1, cell, result)
            return carry

        lax.fori_loop(0, half_cells // GROUP, body, 0)

    def first_faces(part):
        def body(index, carry):
            for inner in range(GROUP):
                cell = half_cells * part + index * GROUP + inner
                store_faces(0, cell, start_ref[cell])
            return carry

        lax.fori_loop(0, half_cells // GROUP, body, 0)

    for part in (0, 1):
        first_faces(part)
        copy_of(0, part).start()
    order = (1, 0)
    for step in range(steps):
        for part in order:
            copy_of(step, 1 - part).wait_recv()
            work(step, part)
            if step + 1 < steps:
                copy_of(step + 1, part).start()
        order = order[::-1]
    for step in range(steps):
        for part in (0, 1):
            copy_of(step, part).wait_send()


def chain(start, neighbours, coefs, weight, comb, pick, steps, plain, ident):
    count = lax.axis_size("domain")
    cells, _, columns = start.shape
    half_cells = cells // 2
    vmem = pl.BlockSpec(memory_space=pltpu.VMEM)
    smem = pl.BlockSpec(memory_space=pltpu.SMEM)
    field = pltpu.VMEM(start.shape, jnp.bfloat16)
    rim = pltpu.VMEM((half_cells, FACE, columns), jnp.bfloat16)
    return pl.pallas_call(
        functools.partial(chain_kernel, steps, plain, count, half_cells),
        out_shape=jax.ShapeDtypeStruct(start.shape, jnp.bfloat16),
        in_specs=[smem, smem, vmem, vmem, vmem, vmem],
        out_specs=vmem,
        scratch_shapes=[field] * (steps - 1)
        + [pltpu.VMEM((6, cells, FACE, columns), jnp.bfloat16)] * steps
        + [rim] * (2 * steps)
        + [pltpu.SemaphoreType.DMA((steps, 2)), pltpu.SemaphoreType.DMA((steps, 2))],
        compiler_params=pltpu.CompilerParams(
            collective_id=ident, has_side_effects=True, vmem_limit_bytes=48 * 2**20
        ),
        cost_estimate=pl.CostEstimate(
            flops=steps * cells * 2 * columns * ROWS * 512,
            bytes_accessed=steps * 16 * 2**20,
            transcendentals=0,
        ),
        name="chain" if not plain else "image",
    )(neighbours, coefs, start, weight, comb, pick)


def factor_inverse(block):
    lanes = lax.broadcasted_iota(jnp.int32, (8, BLOCK), 1)
    subs = lax.broadcasted_iota(jnp.int32, (8, BLOCK), 0)
    tiles = [block[8 * t : 8 * t + 8] for t in range(BLOCK // 8)]
    done = [jnp.zeros((8, BLOCK), jnp.float32) for _ in tiles]
    for j in range(0, BLOCK, PIVOTS):
        at, within = divmod(j, 8)
        own = range(PIVOTS)
        raw = [
            jnp.broadcast_to(tiles[at][within + s : within + s + 1], (8, BLOCK)) for s in own
        ]
        entry = [
            [jnp.broadcast_to(raw[s][:, j + t : j + t + 1], (8, BLOCK)) for t in range(s + 1)]
            for s in own
        ]
        here = (lanes >= j) & (lanes < j + PIVOTS)
        rows = [jnp.where(lanes == j + s, 1.0, jnp.where(here, 0.0, raw[s])) for s in own]
        inv = []
        ratio = [[None] * PIVOTS for _ in own]
        for t in own:
            inv.append(1.0 / entry[t][t])
            final = jnp.where(lanes <= j + t, rows[t], 0.0) * lax.rsqrt(entry[t][t])
            done[at] = jnp.where(subs == within + t, final, done[at])
            for s in range(t + 1, PIVOTS):
                ratio[s][t] = entry[s][t] * inv[t]
            for s in range(t + 1, PIVOTS):
                for q in range(t + 1, s + 1):
                    entry[s][q] = entry[s][q] - ratio[s][t] * entry[q][t]
                rows[s] = rows[s] - ratio[s][t] * rows[t]
        solved = [rows[t] * inv[t] for t in own]
        for t in reversed(own):
            for s in range(t):
                solved[s] = solved[s] - ratio[t][s] * solved[t]
        for t in range(at, BLOCK // 8):
            if t == at and within + PIVOTS == 8:
                continue
            tile = tiles[t]
            fresh = jnp.where(here, 0.0, tile)
            for s in own:
                fresh = fresh - jnp.broadcast_to(tile[:, j + s : j + s + 1], (8, BLOCK)) * solved[s]
            tiles[t] = jnp.where(subs >= within + PIVOTS, fresh, tile) if t == at else fresh
    return jnp.concatenate(done, axis=0)


def inverse_kernel(first, last, source_ref, out_ref, row_ref):
    size = source_ref.shape[0]
    blocks = size // BLOCK
    out_ref[...] = source_ref[...]
    rows_of = lax.broadcasted_iota(jnp.int32, (BLOCK, BLOCK), 0)
    lanes_of = lax.broadcasted_iota(jnp.int32, (BLOCK, BLOCK), 1)
    eye = (rows_of == lanes_of).astype(jnp.float32)
    column_ids = lax.broadcasted_iota(jnp.int32, (BLOCK, size), 1)

    def step(k, carry):
        base = pl.multiple_of(k * BLOCK, BLOCK)
        own = pl.ds(base, BLOCK)
        small = factor_inverse(out_ref[own, own])
        out_ref[own, own] = eye
        row_ref[...] = jnp.dot(
            small, out_ref[own, :], precision=highest, preferred_element_type=jnp.float32
        )
        out_ref[own, :] = jnp.where(column_ids < base + BLOCK, row_ref[...], 0.0)

        def update(i, inner):
            low = pl.ds(pl.multiple_of(i * BLOCK, BLOCK), BLOCK)
            out_ref[low, own] = jnp.zeros((BLOCK, BLOCK), jnp.float32)
            out_ref[low, :] = out_ref[low, :] - lax.dot_general(
                row_ref[:, low],
                row_ref[...],
                (((0,), (0,)), ((), ())),
                precision=highest,
                preferred_element_type=jnp.float32,
            )
            return inner

        return lax.fori_loop(k + 1, blocks, update, carry)

    lax.fori_loop(first, last, step, 0)


def cholesky_inverse(margin, first, last):
    size = margin.shape[0]
    return pl.pallas_call(
        functools.partial(inverse_kernel, first, last),
        out_shape=jax.ShapeDtypeStruct(margin.shape, jnp.float32),
        in_specs=[pl.BlockSpec(memory_space=pltpu.VMEM)],
        out_specs=pl.BlockSpec(memory_space=pltpu.VMEM),
        scratch_shapes=[pltpu.VMEM((BLOCK, size), jnp.float32)],
        compiler_params=pltpu.CompilerParams(vmem_limit_bytes=40 * 2**20),
        cost_estimate=pl.CostEstimate(
            flops=75 * size**3, bytes_accessed=8 * size * size, transcendentals=size
        ),
        name="cholesky_inverse",
    )(margin)


def per_device(wavefunctions, potential, cell_matrix, neighbours, window):
    cells = neighbours.shape[0]
    nodes, columns = wavefunctions.shape
    wide = cell_matrix.astype(jnp.float32)
    stiffness = ((wide + wide.T) * 0.5).astype(jnp.bfloat16)
    table = face_table()
    pad = ROWS - NPC
    comb = jnp.concatenate(
        [jnp.pad(stiffness, ((0, pad), (0, pad))), jnp.asarray(-penalty * table, jnp.bfloat16)],
        axis=1,
    )
    pick = jnp.asarray(table.T, jnp.bfloat16)
    weight = (
        jnp.pad(potential.reshape(cells, NPC), ((0, 0), (0, pad)))
        + penalty * jnp.asarray(table.sum(axis=1))[None, :]
    )[:, :, None]
    center = (window[0] + window[1]) * 0.5
    half = (window[1] - window[0]) * 0.5
    coefs = jnp.stack([center, 1.0 / half, 2.0 / half])
    start = jnp.pad(wavefunctions.reshape(cells, NPC, columns), ((0, 0), (0, pad), (0, 0)))
    common = (neighbours, coefs, weight, comb, pick)
    last = chain(start, *common, 4, False, 0)
    gathered = lax.all_gather(last.reshape(cells * ROWS, columns), "band", axis=0)
    image = chain(last, *common, 1, True, 1).reshape(cells * ROWS, columns)
    last = last.reshape(cells * ROWS, columns)
    bands = gathered.shape[0]
    size = bands * columns

    total_rows = nodes * lax.axis_size("domain")
    contract = (((0,), (0,)), ((), ()))
    margin_part = jnp.concatenate(
        [
            lax.dot_general(last, gathered[b], contract, preferred_element_type=jnp.float32)
            for b in range(bands)
        ],
        axis=1,
    )
    margin_rows = lax.psum(margin_part, "domain")
    margin = lax.all_gather(margin_rows / total_rows, "band", axis=0, tiled=True)
    image, margin = lax.optimization_barrier((image, margin))
    cross_part = jnp.einsum(
        "bni,nj->bij", gathered, image, preferred_element_type=jnp.float32
    ).reshape(size, columns)
    cross_cols = lax.psum(cross_part, "domain")
    blocks = size // BLOCK
    begun = cholesky_inverse(margin, 0, blocks // 2)
    cross_cols, begun = lax.optimization_barrier((cross_cols, begun))
    cross = lax.all_gather(cross_cols / total_rows, "band", axis=0)
    inverse = cholesky_inverse(begun, blocks // 2, blocks)
    mine = lax.dynamic_slice_in_dim(inverse, lax.axis_index("band") * columns, columns, 0)
    filtered = jnp.einsum(
        "bnj,kbj->nk",
        gathered,
        mine.astype(jnp.bfloat16).reshape(columns, bands, columns),
        preferred_element_type=jnp.float32,
    ).astype(jnp.bfloat16)
    filtered = filtered.reshape(cells, ROWS, columns)[:, :NPC].reshape(nodes, columns)
    left = jnp.einsum(
        "ik,bkj->ibj", mine, cross, precision=highest, preferred_element_type=jnp.float32
    ).reshape(columns, size)
    projected = lax.dot_general(
        left,
        inverse,
        (((1,), (1,)), ((), ())),
        precision=highest,
        preferred_element_type=jnp.float32,
    )
    return (filtered, projected)


def solution(mesh):
    placed = (P("domain", "band"), P("domain"), P(), P("domain", None), P())
    return jax.shard_map(
        per_device,
        mesh=mesh,
        in_specs=placed,
        out_specs=(P("domain", "band"), P("band", None)),
        check_vma=False,
    )
```

```python
import functools

import jax
import jax.numpy as jnp
import numpy as np
from jax import lax
from jax.experimental import pallas as pl
from jax.experimental.pallas import tpu as pltpu
from jax.sharding import PartitionSpec as P

NPC = 125
ROWS = 128
FACE = 32
GROUP = 4
BLOCK = 128
PIVOTS = 4
penalty = 0.5
highest = lax.Precision.HIGHEST
MESH = pl.DeviceIdType.MESH


def face_table():
    incidence = np.zeros((ROWS, 6 * FACE), np.float32)
    for direction in range(6):
        axis_index = direction // 2
        level = 4 * (direction % 2)
        for first in range(5):
            for second in range(5):
                others = [first, second]
                coords = others[:axis_index] + [level] + others[axis_index:]
                node = 25 * coords[0] + 5 * coords[1] + coords[2]
                incidence[node, FACE * direction + 5 * first + second] = 1.0
    return incidence


def chain_kernel(steps, plain, count, half_cells, *refs):
    nb_ref, coef_ref, start_ref, weight_ref, comb_ref, pick_ref, out_ref = refs[:7]
    rest = list(refs[7:])
    fields = [start_ref] + rest[: steps - 1] + [out_ref]
    rest = rest[steps - 1 :]
    faces, below, above = rest[:steps], rest[steps : 2 * steps], rest[2 * steps : 3 * steps]
    send_sem, recv_sem = rest[3 * steps :]
    me = lax.axis_index("domain")
    up, down = lax.rem(me + 1, count), lax.rem(me + count - 1, count)

    barrier = pltpu.get_barrier_semaphore()
    for other in (down, up):
        pl.semaphore_signal(barrier, inc=1, device_id={"domain": other}, device_id_type=MESH)
    pl.semaphore_wait(barrier, 2)

    def copy_of(step, part):
        return pltpu.make_async_remote_copy(
            src_ref=faces[step].at[4 + part, pl.ds(half_cells * part, half_cells)],
            dst_ref=(below if part else above)[step],
            send_sem=send_sem.at[step, part],
            recv_sem=recv_sem.at[step, part],
            device_id={"domain": up if part else down},
            device_id_type=MESH,
        )

    def store_faces(step, cell, value):
        picked = jnp.dot(pick_ref[...], value, preferred_element_type=jnp.float32)
        picked = picked.astype(jnp.bfloat16)
        for d in range(6):
            faces[step][d, cell] = picked[FACE * d : FACE * (d + 1)]

    center = coef_ref[0]

    def work(step, part):
        scale = 1.0 if plain else coef_ref[1 if step == 0 else 2]
        shift = 0.0 if plain else center
        now, later = fields[step], fields[step + 1]
        before = fields[step - 1] if step > 0 else None

        def body(index, carry):
            for inner in range(GROUP):
                cell = half_cells * part + index * GROUP + inner
                value = now[cell]
                pieces = [value]
                for d in range(6):
                    slot = nb_ref[cell, d]
                    if d == 4 and part == 0:
                        pieces.append(below[step][lax.rem(slot, half_cells)])
                    elif d == 5 and part == 1:
                        pieces.append(above[step][lax.rem(slot, half_cells)])
                    else:
                        pieces.append(faces[step][d ^ 1, slot])
                stacked = jnp.concatenate(pieces, axis=0)
                image = jnp.dot(comb_ref[...], stacked, preferred_element_type=jnp.float32)
                wide = value.astype(jnp.float32)
                if plain:
                    image = image + weight_ref[cell] * wide
                else:
                    image = image * scale + ((weight_ref[cell] - shift) * scale) * wide
                if before is not None:
                    image = image - before[cell].astype(jnp.float32)
                result = image.astype(jnp.bfloat16)
                later[cell] = result
                if step + 1 < steps:
                    store_faces(step + 1, cell, result)
            return carry

        lax.fori_loop(0, half_cells // GROUP, body, 0)

    def first_faces(part):
        def body(index, carry):
            for inner in range(GROUP):
                cell = half_cells * part + index * GROUP + inner
                store_faces(0, cell, start_ref[cell])
            return carry

        lax.fori_loop(0, half_cells // GROUP, body, 0)

    for part in (0, 1):
        first_faces(part)
        copy_of(0, part).start()
    order = (1, 0)
    for step in range(steps):
        for part in order:
            copy_of(step, 1 - part).wait_recv()
            work(step, part)
            if step + 1 < steps:
                copy_of(step + 1, part).start()
        order = order[::-1]
    for step in range(steps):
        for part in (0, 1):
            copy_of(step, part).wait_send()


def chain(start, neighbours, coefs, weight, comb, pick, steps, plain, ident):
    count = lax.axis_size("domain")
    cells, _, columns = start.shape
    half_cells = cells // 2
    vmem = pl.BlockSpec(memory_space=pltpu.VMEM)
    smem = pl.BlockSpec(memory_space=pltpu.SMEM)
    field = pltpu.VMEM(start.shape, jnp.bfloat16)
    rim = pltpu.VMEM((half_cells, FACE, columns), jnp.bfloat16)
    return pl.pallas_call(
        functools.partial(chain_kernel, steps, plain, count, half_cells),
        out_shape=jax.ShapeDtypeStruct(start.shape, jnp.bfloat16),
        in_specs=[smem, smem, vmem, vmem, vmem, vmem],
        out_specs=vmem,
        scratch_shapes=[field] * (steps - 1)
        + [pltpu.VMEM((6, cells, FACE, columns), jnp.bfloat16)] * steps
        + [rim] * (2 * steps)
        + [pltpu.SemaphoreType.DMA((steps, 2)), pltpu.SemaphoreType.DMA((steps, 2))],
        compiler_params=pltpu.CompilerParams(
            collective_id=ident, has_side_effects=True, vmem_limit_bytes=48 * 2**20
        ),
        cost_estimate=pl.CostEstimate(
            flops=steps * cells * 2 * columns * ROWS * 512,
            bytes_accessed=steps * 16 * 2**20,
            transcendentals=0,
        ),
        name="chain" if not plain else "image",
    )(neighbours, coefs, start, weight, comb, pick)


def factor_inverse(block):
    lanes = lax.broadcasted_iota(jnp.int32, (8, BLOCK), 1)
    subs = lax.broadcasted_iota(jnp.int32, (8, BLOCK), 0)
    tiles = [block[8 * t : 8 * t + 8] for t in range(BLOCK // 8)]
    done = [jnp.zeros((8, BLOCK), jnp.float32) for _ in tiles]
    for j in range(0, BLOCK, PIVOTS):
        at, within = divmod(j, 8)
        own = range(PIVOTS)
        raw = [
            jnp.broadcast_to(tiles[at][within + s : within + s + 1], (8, BLOCK)) for s in own
        ]
        entry = [
            [jnp.broadcast_to(raw[s][:, j + t : j + t + 1], (8, BLOCK)) for t in range(s + 1)]
            for s in own
        ]
        here = (lanes >= j) & (lanes < j + PIVOTS)
        rows = [jnp.where(lanes == j + s, 1.0, jnp.where(here, 0.0, raw[s])) for s in own]
        inv = []
        ratio = [[None] * PIVOTS for _ in own]
        for t in own:
            inv.append(1.0 / entry[t][t])
            final = jnp.where(lanes <= j + t, rows[t], 0.0) * lax.rsqrt(entry[t][t])
            done[at] = jnp.where(subs == within + t, final, done[at])
            for s in range(t + 1, PIVOTS):
                ratio[s][t] = entry[s][t] * inv[t]
            for s in range(t + 1, PIVOTS):
                for q in range(t + 1, s + 1):
                    entry[s][q] = entry[s][q] - ratio[s][t] * entry[q][t]
                rows[s] = rows[s] - ratio[s][t] * rows[t]
        solved = [rows[t] * inv[t] for t in own]
        for t in reversed(own):
            for s in range(t):
                solved[s] = solved[s] - ratio[t][s] * solved[t]
        for t in range(at, BLOCK // 8):
            if t == at and within + PIVOTS == 8:
                continue
            tile = tiles[t]
            fresh = jnp.where(here, 0.0, tile)
            for s in own:
                fresh = fresh - jnp.broadcast_to(tile[:, j + s : j + s + 1], (8, BLOCK)) * solved[s]
            tiles[t] = jnp.where(subs >= within + PIVOTS, fresh, tile) if t == at else fresh
    return jnp.concatenate(done, axis=0)


def inverse_kernel(first, last, source_ref, out_ref, row_ref):
    size = source_ref.shape[0]
    blocks = size // BLOCK
    out_ref[...] = source_ref[...]
    rows_of = lax.broadcasted_iota(jnp.int32, (BLOCK, BLOCK), 0)
    lanes_of = lax.broadcasted_iota(jnp.int32, (BLOCK, BLOCK), 1)
    eye = (rows_of == lanes_of).astype(jnp.float32)
    column_ids = lax.broadcasted_iota(jnp.int32, (BLOCK, size), 1)

    def step(k, carry):
        base = pl.multiple_of(k * BLOCK, BLOCK)
        own = pl.ds(base, BLOCK)
        small = factor_inverse(out_ref[own, own])
        out_ref[own, own] = eye
        row_ref[...] = jnp.dot(
            small, out_ref[own, :], precision=highest, preferred_element_type=jnp.float32
        )
        out_ref[own, :] = jnp.where(column_ids < base + BLOCK, row_ref[...], 0.0)

        def update(i, inner):
            low = pl.ds(pl.multiple_of(i * BLOCK, BLOCK), BLOCK)
            out_ref[low, own] = jnp.zeros((BLOCK, BLOCK), jnp.float32)
            out_ref[low, :] = out_ref[low, :] - lax.dot_general(
                row_ref[:, low],
                row_ref[...],
                (((0,), (0,)), ((), ())),
                precision=highest,
                preferred_element_type=jnp.float32,
            )
            return inner

        return lax.fori_loop(k + 1, blocks, update, carry)

    lax.fori_loop(first, last, step, 0)


def cholesky_inverse(margin, first, last):
    size = margin.shape[0]
    return pl.pallas_call(
        functools.partial(inverse_kernel, first, last),
        out_shape=jax.ShapeDtypeStruct(margin.shape, jnp.float32),
        in_specs=[pl.BlockSpec(memory_space=pltpu.VMEM)],
        out_specs=pl.BlockSpec(memory_space=pltpu.VMEM),
        scratch_shapes=[pltpu.VMEM((BLOCK, size), jnp.float32)],
        compiler_params=pltpu.CompilerParams(vmem_limit_bytes=40 * 2**20),
        cost_estimate=pl.CostEstimate(
            flops=90 * size**3, bytes_accessed=8 * size * size, transcendentals=size
        ),
        name="cholesky_inverse",
    )(margin)


def per_device(wavefunctions, potential, cell_matrix, neighbours, window):
    cells = neighbours.shape[0]
    nodes, columns = wavefunctions.shape
    wide = cell_matrix.astype(jnp.float32)
    stiffness = ((wide + wide.T) * 0.5).astype(jnp.bfloat16)
    table = face_table()
    pad = ROWS - NPC
    comb = jnp.concatenate(
        [jnp.pad(stiffness, ((0, pad), (0, pad))), jnp.asarray(-penalty * table, jnp.bfloat16)],
        axis=1,
    )
    pick = jnp.asarray(table.T, jnp.bfloat16)
    weight = (
        jnp.pad(potential.reshape(cells, NPC), ((0, 0), (0, pad)))
        + penalty * jnp.asarray(table.sum(axis=1))[None, :]
    )[:, :, None]
    center = (window[0] + window[1]) * 0.5
    half = (window[1] - window[0]) * 0.5
    coefs = jnp.stack([center, 1.0 / half, 2.0 / half])
    start = jnp.pad(wavefunctions.reshape(cells, NPC, columns), ((0, 0), (0, pad), (0, 0)))
    common = (neighbours, coefs, weight, comb, pick)
    last = chain(start, *common, 4, False, 0)
    gathered = lax.all_gather(last.reshape(cells * ROWS, columns), "band", axis=0)
    image = chain(last, *common, 1, True, 1).reshape(cells * ROWS, columns)
    last = last.reshape(cells * ROWS, columns)
    bands = gathered.shape[0]
    size = bands * columns

    total_rows = nodes * lax.axis_size("domain")
    contract = (((0,), (0,)), ((), ()))
    margin_part = jnp.concatenate(
        [
            lax.dot_general(last, gathered[b], contract, preferred_element_type=jnp.float32)
            for b in range(bands)
        ],
        axis=1,
    )
    margin_rows = lax.psum(margin_part, "domain")
    margin = lax.all_gather(margin_rows / total_rows, "band", axis=0, tiled=True)
    cross_part = jnp.einsum(
        "bni,nj->bij", gathered, image, preferred_element_type=jnp.float32
    ).reshape(size, columns)
    cross_part, margin = lax.optimization_barrier((cross_part, margin))
    cross_cols = lax.psum(cross_part, "domain")
    inverse = cholesky_inverse(margin, 0, size // BLOCK)
    cross_cols, inverse = lax.optimization_barrier((cross_cols, inverse))
    mine = lax.dynamic_slice_in_dim(inverse, lax.axis_index("band") * columns, columns, 0)
    filtered = jnp.einsum(
        "bnj,kbj->nk",
        gathered,
        mine.astype(jnp.bfloat16).reshape(columns, bands, columns),
        preferred_element_type=jnp.float32,
    ).astype(jnp.bfloat16)
    filtered = filtered.reshape(cells, ROWS, columns)[:, :NPC].reshape(nodes, columns)
    left_cols = jnp.dot(
        inverse, cross_cols / total_rows, precision=highest, preferred_element_type=jnp.float32
    )
    left = lax.all_to_all(left_cols, "band", split_axis=0, concat_axis=1, tiled=True)
    projected = lax.dot_general(
        left,
        inverse,
        (((1,), (1,)), ((), ())),
        precision=highest,
        preferred_element_type=jnp.float32,
    )
    return (filtered, projected)


def solution(mesh):
    placed = (P("domain", "band"), P("domain"), P(), P("domain", None), P())
    return jax.shard_map(
        per_device,
        mesh=mesh,
        in_specs=placed,
        out_specs=(P("domain", "band"), P("band", None)),
        check_vma=False,
    )
```
